32 devices in a mesh: parts: 2 (over y), own: 4 (over z), sub: 2 (over x), rep: 2 (over core).
Axes of the slice: x: 2, y: 2, z: 4, core: 2. Of those that a mesh axis runs over, the one named last changes fastest.
Arguments:
- density: float32 [256, 256, 256], P(('parts', 'own', 'sub', 'rep')), parts along dimension 0, may hold values from 0 to 1
- tile_coords: int32 [256, 4], P(('parts', 'own', 'sub', 'rep')), parts along dimension 0, may hold values from -1 to 31, as said below
- neighbours: int32 [256, 8], P(('parts', 'own', 'sub', 'rep')), parts along dimension 0, may hold values from -1 to 127, as said below
- rate_constants: float32 [20], P('parts'), parts along dimension 0, may hold values from 0.05 to 0.5, as said below
Outputs:
- density_next: float32 [256, 256, 256], P(('parts', 'own', 'sub', 'rep')), parts along dimension 0
The draws below stay inside these ranges and needn't reach their ends.
There are 2 independent parts, one for each index of `parts`. The reference program is written for one: setup_inputs(seed, part) draws one part's arguments, and reference() takes and returns one part's arrays. A program takes and returns all parts, laid end to end along the dimension named above; each array names one. Nothing has to cross between parts.
Inputs may be any that keep to these rules, and one draw needn't show every extreme that they name: `tile_coords`: slots come in groups of 8, one group a device, ordered by own, then sub, then rep index. The tile (t1, t2, t3, t4) lies on the device with own index t1, sub index t3 // 2 and rep index t4 // 2, and no tile twice. A device's active tiles fill its first slots; the other slots hold -1 in all four entries. Every device holds 1 to 8 active tiles and some device holds 8. `neighbours`: entry (g, 2k) is the slot of the active tile one lower along species k + 1 than slot g's tile, entry (g, 2k + 1) that of the one one higher, for k = 0 to 3; -1 where that tile is not active or slot g is empty. `rate_constants`: entries 0 and 5 lie in [0.05, 0.25], 1 and 6 in [0.05, 0.25], 2 and 7 in [0.05, 0.2], 3 and 8 in [0.05, 0.25], 4 and 9 in [0.1, 0.5].
All inputs are finite; a program needn't handle non-finite values.
Results may differ from the reference program's by a relative error of at most 0.00002.
Values sent between devices are 32-bit elements; how exact they have to be, the bound alone decides.
A program may use at most 128 MiB of HBM per device.

```python
import math
import jax
import jax.numpy as jnp
from jax import lax

E = 16
TB = 32
C_DEV = 2
D_DEV = 2
SLOTS = 8
RATES = 10
N1 = 512
N2 = 512
N3 = 256
N4 = 256
TA = 4
TC = 4
TD = 4
SLOTS_ALL = 128


def tile_layout(key):
    owners = TA
    sub_count = TC // C_DEV
    rep_count = TD // D_DEV
    devices = owners * sub_count * rep_count
    light_most = SLOTS // 2
    pair_count = owners // 2
    subkeys = jax.random.split(key, 6)
    heavy_side = jax.random.randint(subkeys[0], (pair_count, sub_count, rep_count), 0, 2)
    heavy_side = heavy_side.at[pair_count - 1, sub_count - 1, rep_count - 1].set(1)
    upper_half = (jnp.arange(owners) >= pair_count).astype(jnp.int32)
    side_full = jnp.concatenate([heavy_side, heavy_side], axis=0)
    overloaded = side_full == upper_half[:, None, None]
    heavy_total = jax.random.randint(subkeys[1], (owners, sub_count, rep_count), light_most + 1, SLOTS + 1)
    light_total = jax.random.randint(subkeys[2], (owners, sub_count, rep_count), 1, light_most + 1)
    tile_total = jnp.where(overloaded, heavy_total, light_total)
    tile_total = tile_total.at[owners - 1, sub_count - 1, rep_count - 1].set(SLOTS)
    tile_total = tile_total.at[pair_count - 1, sub_count - 1, rep_count - 1].set(light_most)
    tile_total = tile_total.reshape(devices)
    slot_index = jnp.arange(SLOTS, dtype=jnp.int32)
    scores = jax.random.randint(subkeys[3], (devices, 8), 0, 1 << 20) * 8 + jnp.arange(8, dtype=jnp.int32)
    offset_order = jnp.argsort(scores, axis=1)[:, :SLOTS].astype(jnp.int32)
    offset_order = offset_order.at[devices - 1].set(7 - slot_index)
    shift_b = offset_order // 4 % 2
    shift_c = offset_order // 2 % 2
    shift_d = offset_order % 2
    centre_b = jax.random.randint(subkeys[4], (), 0, TB - 2)
    start_b = centre_b + jax.random.randint(subkeys[5], (devices,), 0, 2)
    start_b = jnp.minimum(start_b, TB - 2)
    start_b = start_b.at[devices - 1].set(TB - 2)
    device_index = jnp.arange(devices, dtype=jnp.int32)
    own_index = device_index // (sub_count * rep_count)
    sub_index = device_index // rep_count % sub_count
    rep_index = device_index % rep_count
    coord_one = jnp.broadcast_to(own_index[:, None], (devices, SLOTS))
    coord_two = start_b[:, None] + shift_b
    coord_three = sub_index[:, None] * C_DEV + shift_c
    coord_four = rep_index[:, None] * D_DEV + shift_d
    coords = jnp.stack([coord_one, coord_two, coord_three, coord_four], axis=-1)
    living = slot_index[None, :] < tile_total[:, None]
    coords = jnp.where(living[:, :, None], coords, -1).astype(jnp.int32)
    flat_coords = coords.reshape(devices * SLOTS, 4)
    step_table = jnp.array([[-1, 0, 0, 0], [1, 0, 0, 0], [0, -1, 0, 0], [0, 1, 0, 0], [0, 0, -1, 0], [0, 0, 1, 0], [0, 0, 0, -1], [0, 0, 0, 1]], jnp.int32)
    target = flat_coords[:, None, :] + step_table[None, :, :]
    limits = jnp.array([TA, TB, TC, TD], jnp.int32)
    inside = jnp.all((target >= 0) & (target < limits), axis=-1) & (flat_coords[:, None, 0] >= 0)
    home_device = (target[..., 0] * sub_count + target[..., 2] // C_DEV) * rep_count + target[..., 3] // D_DEV
    home_device = jnp.clip(home_device, 0, devices - 1)
    candidates = coords[home_device]
    matches = jnp.all(candidates == target[:, :, None, :], axis=-1)
    located = jnp.any(matches, axis=-1) & inside
    position = jnp.sum(jnp.where(matches, slot_index, 0), axis=-1)
    neighbour_slots = jnp.where(located, home_device * SLOTS + position, -1).astype(jnp.int32)
    return (flat_coords, neighbour_slots)


def draw_tile_coords(key, part):
    flat_coords, neighbour_slots = tile_layout(key)
    return flat_coords


def draw_neighbours(key, part):
    flat_coords, neighbour_slots = tile_layout(key)
    return neighbour_slots


def draw_rate_constants(key, part):
    key = jax.random.fold_in(key, 7)
    lowest = jnp.array([0.05, 0.05, 0.05, 0.05, 0.1, 0.05, 0.05, 0.05, 0.05, 0.1], jnp.float32)
    highest = jnp.array([0.25, 0.25, 0.2, 0.25, 0.5, 0.25, 0.25, 0.2, 0.25, 0.5], jnp.float32)
    uniform_draw = jax.random.uniform(key, (RATES,), jnp.float32)
    return jnp.exp(jnp.log(lowest) + uniform_draw * (jnp.log(highest) - jnp.log(lowest)))


def block_levels(rng, shape, cuts, low, high):
    gain = 1.0
    for dim, shards_of in cuts:
        heights = jax.random.uniform(jax.random.fold_in(jax.random.fold_in(rng, 6), dim), (shards_of,), jnp.float32, low / len(cuts), high / len(cuts))
        gain = gain * jnp.repeat(jnp.exp(heights), shape[dim] // shards_of).reshape((-1,) + (1,) * (len(shape) - 1 - dim))
    return gain


def setup_inputs(seed: int = 0, part: int = 0) -> dict:
    key_of = jax.random.split(jax.random.key(seed), 5)
    part_keys = jax.random.split(jax.random.fold_in(key_of[4], part), 5)
    density = jnp.clip(1.0 * jax.random.uniform(part_keys[0], (SLOTS_ALL, E * E, E * E), jnp.float32) ** block_levels(part_keys[0], (SLOTS_ALL, E * E, E * E), ((0, 16),), -0.2, 0.2), 0.0, 1.0)
    tile_coords = draw_tile_coords(jax.random.fold_in(jax.random.fold_in(key_of[4], part), 71), part)
    neighbours = draw_neighbours(jax.random.fold_in(jax.random.fold_in(key_of[4], part), 71), part)
    rate_constants = draw_rate_constants(jax.random.fold_in(jax.random.fold_in(key_of[4], part), 71), part)
    return {"density": density, "tile_coords": tile_coords, "neighbours": neighbours, "rate_constants": rate_constants}


def layers(values, tile_edge):
    slot_count = values.shape[0]
    tile_area = tile_edge * tile_edge
    by_cells = values.reshape(slot_count, tile_area, tile_edge, tile_edge)
    by_rows = values.reshape(slot_count, tile_edge, tile_edge, tile_area)
    return (values[:, :tile_edge, :], values[:, tile_area - tile_edge:, :], by_rows[:, :, 0, :], by_rows[:, :, tile_edge - 1, :], jnp.swapaxes(by_cells[:, :, 0, :], 1, 2), jnp.swapaxes(by_cells[:, :, tile_edge - 1, :], 1, 2), jnp.swapaxes(by_cells[:, :, :, 0], 1, 2), jnp.swapaxes(by_cells[:, :, :, tile_edge - 1], 1, 2))

def generator(values, face_set, coords, rate_constants, extents):
    tile_area = values.shape[1]
    tile_edge = math.isqrt(tile_area)
    row_index = lax.broadcasted_iota(jnp.int32, (1, tile_area, tile_area), 1)
    col_index = lax.broadcasted_iota(jnp.int32, (1, tile_area, tile_area), 2)
    row_high = row_index // tile_edge
    row_low = row_index % tile_edge
    col_high = col_index // tile_edge
    col_low = col_index % tile_edge
    anchor = (coords * tile_edge).astype(jnp.float32)[:, :, None, None]
    extent_one, extent_two, extent_three, extent_four = extents
    level_one = anchor[:, 0] + row_high.astype(jnp.float32)
    level_two = anchor[:, 1] + row_low.astype(jnp.float32)
    level_three = anchor[:, 2] + col_high.astype(jnp.float32)
    level_four = anchor[:, 3] + col_low.astype(jnp.float32)
    share_one = level_one / extent_one
    share_two = level_two / extent_two
    share_three = level_three / extent_three
    share_four = level_four / extent_four
    below_one = jnp.where(row_high == 0, jnp.tile(face_set[0], (1, tile_edge, 1)), jnp.roll(values, tile_edge, axis=1))
    above_one = jnp.where(row_high == tile_edge - 1, jnp.tile(face_set[1], (1, tile_edge, 1)), jnp.roll(values, -tile_edge, axis=1))
    below_two = jnp.where(row_low == 0, jnp.repeat(face_set[2], tile_edge, axis=1), jnp.roll(values, 1, axis=1))
    above_two = jnp.where(row_low == tile_edge - 1, jnp.repeat(face_set[3], tile_edge, axis=1), jnp.roll(values, -1, axis=1))
    below_three = jnp.where(col_high == 0, jnp.tile(jnp.swapaxes(face_set[4], 1, 2), (1, 1, tile_edge)), jnp.roll(values, tile_edge, axis=2))
    above_three = jnp.where(col_high == tile_edge - 1, jnp.tile(jnp.swapaxes(face_set[5], 1, 2), (1, 1, tile_edge)), jnp.roll(values, -tile_edge, axis=2))
    below_four = jnp.where(col_low == 0, jnp.repeat(jnp.swapaxes(face_set[6], 1, 2), tile_edge, axis=2), jnp.roll(values, 1, axis=2))
    above_four = jnp.where(col_low == tile_edge - 1, jnp.repeat(jnp.swapaxes(face_set[7], 1, 2), tile_edge, axis=2), jnp.roll(values, -1, axis=2))
    ratio_two = share_two / rate_constants[4]
    ratio_one = share_one / rate_constants[9]
    transcribe_first = rate_constants[0] / (1.0 + ratio_two * ratio_two)
    transcribe_second = rate_constants[5] / (1.0 + ratio_one * ratio_one)
    outflow = transcribe_first + rate_constants[1] * share_three + rate_constants[2] * share_three + rate_constants[3] * share_one + transcribe_second + rate_constants[6] * share_four + rate_constants[7] * share_four + rate_constants[8] * share_two
    inflow = transcribe_first * below_three + rate_constants[1] * ((level_three + 1.0) / extent_three) * above_three + rate_constants[2] * share_three * below_one + rate_constants[3] * ((level_one + 1.0) / extent_one) * above_one + transcribe_second * below_four + rate_constants[6] * ((level_four + 1.0) / extent_four) * above_four + rate_constants[7] * share_four * below_two + rate_constants[8] * ((level_two + 1.0) / extent_two) * above_two
    return inflow - outflow * values

def reference(density, tile_coords, neighbours, rate_constants):
    tile_edge = E
    active_mask = (tile_coords[:, 0] >= 0).astype(jnp.float32)[:, None, None]
    initial = density * active_mask
    extents = (float(N1), float(N2), float(N3), float(N4))
    present = neighbours >= 0
    position = jnp.maximum(neighbours, 0)
    block_count = density.shape[0] // SLOTS

    def derivative(values):
        lower_one, upper_one, lower_two, upper_two, lower_three, upper_three, lower_four, upper_four = layers(values, tile_edge)
        sources = (upper_one, lower_one, upper_two, lower_two, upper_three, lower_three, upper_four, lower_four)
        face_set = tuple((jnp.where(present[:, column, None, None], jnp.take(sources[column], position[:, column], axis=0), 0.0) for column in range(8)))
        shaped_values = values.reshape((block_count, SLOTS) + values.shape[1:])
        shaped_faces = tuple((face.reshape((block_count, SLOTS) + face.shape[1:]) for face in face_set))
        shaped_coords = tile_coords.reshape(block_count, SLOTS, 4)

        def one_block(pieces):
            return generator(pieces[0], pieces[1], pieces[2], rate_constants, extents)
        change = lax.map(one_block, (shaped_values, shaped_faces, shaped_coords))
        return change.reshape(values.shape) * active_mask
    rate_one = derivative(initial)
    middle = initial + rate_one
    rate_two = derivative(middle)
    return initial + 0.5 * (rate_one + rate_two)
```

```python
import functools

import jax
import jax.numpy as jnp
from jax import lax
from jax.experimental import pallas as pl
from jax.experimental.pallas import tpu as pltpu
from jax.sharding import PartitionSpec as P

C_DEV = 2
D_DEV = 2
N1 = 512
N2 = 512
N3 = 256
N4 = 256
EDGE = 16
F32 = jnp.float32
MESH = pl.DeviceIdType.MESH

BELOW_ONE, ABOVE_THREE, BELOW_TWO, ABOVE_FOUR, OUT_LANE, LOCAL_ABOVE, LOCAL_BELOW = range(7)
FAR_ABOVE_FOUR, FAR_BELOW_FOUR, FAR_ABOVE_THREE, FAR_BELOW_THREE = range(7, 11)
LANE_ROWS = 11
MAKE_THREE, ABOVE_TWO, OUT_ROW = range(3)
MAKE_FOUR, ABOVE_ONE, OUT_ONE = range(3)


def kernel(counts, x_ref, coord_ref, near_ref, rate_ref, out_ref,
           v, m, y, lane_c, row_c, one_c, pack3, pack4, far1_a, far1_b, far3_a, far3_b, far4_a, far4_b,
           load_sem, store_sem, send1, recv1, send3, recv3, send4, recv4):
    slots = x_ref.shape[0]
    zero_slot = slots
    far1, far3, far4 = (far1_a, far1_b), (far3_a, far3_b), (far4_a, far4_b)
    own_count, sub_count, rep_count = counts
    own = lax.axis_index("own")
    sub = lax.axis_index("sub")
    rep = lax.axis_index("rep")

    loads = [
        pltpu.make_async_copy(x_ref.at[s], v.at[s], load_sem.at[s]) for s in range(slots)
    ]
    for copy in loads:
        copy.start()

    barrier = pltpu.get_barrier_semaphore()
    expected = jnp.int32(0)
    for axis, index, count in (("own", own, own_count), ("sub", sub, sub_count), ("rep", rep, rep_count)):
        for step, there in ((-1, index > 0), (1, index < count - 1)):
            expected = expected + there.astype(jnp.int32)

            @pl.when(there)
            def _():
                pl.semaphore_signal(
                    barrier, inc=1, device_id={axis: index + step}, device_id_type=MESH
                )

    def own_copies(stage, source):
        down = pltpu.make_async_remote_copy(
            src_ref=source.at[pl.ds(0, slots), pl.ds(0, 2)],
            dst_ref=far1[stage].at[1],
            send_sem=send1.at[stage, 0],
            recv_sem=recv1.at[stage, 1],
            device_id={"own": own - 1},
            device_id_type=MESH,
        )
        up = pltpu.make_async_remote_copy(
            src_ref=source.at[pl.ds(0, slots), pl.ds(2 * EDGE - 2, 2)],
            dst_ref=far1[stage].at[0],
            send_sem=send1.at[stage, 1],
            recv_sem=recv1.at[stage, 0],
            device_id={"own": own + 1},
            device_id_type=MESH,
        )
        return (down, own > 0), (up, own < own_count - 1)

    def face_copies(stage, axis, index, count, pack, far, send, recv):
        if count == 2:
            return (
                (
                    pltpu.make_async_remote_copy(
                        src_ref=pack.at[stage, 0],
                        dst_ref=far[stage].at[0],
                        send_sem=send.at[stage, 0],
                        recv_sem=recv.at[stage, 0],
                        device_id={axis: 1 - index},
                        device_id_type=MESH,
                    ),
                    index >= 0,
                ),
            )
        return tuple(
            (
                pltpu.make_async_remote_copy(
                    src_ref=pack.at[stage, side],
                    dst_ref=far[stage].at[1 - side],
                    send_sem=send.at[stage, side],
                    recv_sem=recv.at[stage, 1 - side],
                    device_id={axis: index + 2 * side - 1},
                    device_id_type=MESH,
                ),
                index > 0 if side == 0 else index < count - 1,
            )
            for side in (0, 1)
        )

    def start_all(copies):
        for copy, there in copies:

            @pl.when(there)
            def _():
                copy.start()

    def sub_copies(stage):
        return face_copies(stage, "sub", sub, sub_count, pack3, far3, send3, recv3)

    def rep_copies(stage):
        return face_copies(stage, "rep", rep, rep_count, pack4, far4, send4, recv4)

    def finish(copies):
        for copy, there in copies:

            @pl.when(there)
            def _():
                copy.wait_send()

    def arrivals(copies, flip):
        order = copies[::-1] if flip and len(copies) == 2 else copies
        for (copy, _), (_, there) in zip(order, copies):

            @pl.when(there)
            def _():
                copy.wait_recv()

    lane = lax.broadcasted_iota(jnp.int32, (8, 128), 1)
    sublane = lax.broadcasted_iota(jnp.int32, (8, 128), 0)
    low = lane % EDGE
    rate = [rate_ref[k] for k in range(10)]

    v[zero_slot] = jnp.zeros(v.shape[1:], F32)
    m[zero_slot] = jnp.zeros(m.shape[1:], F32)

    def far_sides(s):
        below_three_far = coord_ref[s, 2] % C_DEV == 0
        below_four_far = coord_ref[s, 3] % D_DEV == 0
        return below_three_far, below_four_far

    def flag(value):
        return jnp.where(value, 1.0, 0.0)

    def coefficients(s, _):
        base = [(coord_ref[s, k] * EDGE).astype(F32) for k in range(4)]
        below_three_far, below_four_far = far_sides(s)
        there = [near_ref[s, k] >= 0 for k in range(8)]
        far_below_three = flag(below_three_far & there[4])
        far_above_three = flag(jnp.logical_not(below_three_far) & there[5])
        far_below_four = flag(below_four_far & there[6])
        far_above_four = flag(jnp.logical_not(below_four_far) & there[7])
        local_below = flag(jnp.logical_not(below_four_far) & there[6])
        local_above = flag(below_four_far & there[7])
        level_four = base[3] + low.astype(F32)
        above_four = rate[6] * ((level_four + 1.0) * (1.0 / N4))
        for h in range(2):
            level_three = base[2] + (lane // EDGE + 8 * h).astype(F32)
            share_three = level_three * (1.0 / N3)
            share_four = level_four * (1.0 / N4)
            above_three = rate[1] * ((level_three + 1.0) * (1.0 / N3))
            cols = pl.ds(128 * h, 128)
            lane_c[s, BELOW_ONE, :, cols] = rate[2] * share_three
            lane_c[s, ABOVE_THREE, :, cols] = above_three
            lane_c[s, BELOW_TWO, :, cols] = rate[7] * share_four
            lane_c[s, ABOVE_FOUR, :, cols] = jnp.where(low == EDGE - 1, 0.0, above_four)
            lane_c[s, OUT_LANE, :, cols] = (
                rate[1] * share_three + rate[2] * share_three
                + rate[6] * share_four + rate[7] * share_four
            )
            lane_c[s, LOCAL_ABOVE, :, cols] = jnp.where(low == EDGE - 1, above_four, 0.0) * local_above
            lane_c[s, LOCAL_BELOW, :, cols] = jnp.where(low == 0, local_below, 0.0)
            lane_c[s, FAR_ABOVE_FOUR, :, cols] = (
                jnp.where(low == EDGE - 1, above_four, 0.0) * far_above_four
            )
            lane_c[s, FAR_BELOW_FOUR, :, cols] = jnp.where(low == 0, far_below_four, 0.0)
            lane_c[s, FAR_ABOVE_THREE, :, cols] = (
                jnp.where(lane >= 128 - EDGE, above_three, 0.0) * far_above_three
            )
            lane_c[s, FAR_BELOW_THREE, :, cols] = jnp.where(lane < EDGE, far_below_three, 0.0)
        for j in range(2):
            level_two = base[1] + (sublane + 8 * j).astype(F32)
            share_two = level_two * (1.0 / N2)
            ratio_two = share_two / rate[4]
            make_three = rate[0] / (1.0 + ratio_two * ratio_two)
            row_c[s, MAKE_THREE, j] = make_three
            row_c[s, ABOVE_TWO, j] = rate[8] * ((level_two + 1.0) * (1.0 / N2))
            row_c[s, OUT_ROW, j] = make_three + rate[8] * share_two

        def by_one(i, _):
            level_one = jnp.full((8, 128), base[0] + i.astype(F32), F32)
            share_one = level_one * (1.0 / N1)
            ratio_one = share_one / rate[9]
            make_four = rate[5] / (1.0 + ratio_one * ratio_one)
            one_c[s, i, MAKE_FOUR] = make_four
            one_c[s, i, ABOVE_ONE] = rate[3] * ((level_one + 1.0) * (1.0 / N1))
            one_c[s, i, OUT_ONE] = make_four + rate[3] * share_one
            return 0

        lax.fori_loop(0, EDGE, by_one, 0)
        return 0

    lax.fori_loop(0, slots, coefficients, 0)

    pl.semaphore_wait(barrier, expected)
    start_all(own_copies(0, x_ref))
    for copy in loads:
        copy.wait()

    def sides_of(index, count):
        return ((0, (index == 0).astype(jnp.int32)),) if count == 2 else ((0, 0), (1, 1))

    def pack_into(stage, rows, gathered):
        for where, side in sides_of(sub, sub_count):
            for j in range(2):
                total = jnp.zeros((8, 128), F32)
                for s in range(slots):
                    cells = jnp.where(side == 1, gathered[s][j][1], gathered[s][j][0])
                    turned = pltpu.roll(cells, (EDGE * s + EDGE * side) % 128, 1)
                    total = jnp.where(lane // EDGE == s, turned, total)
                pack3[stage, where, rows + j] = total
        for where, side in sides_of(rep, rep_count):
            for j in range(2):
                total = jnp.zeros((8, 128), F32)
                for s in range(slots):
                    for h in range(2):
                        turned = pltpu.roll(
                            gathered[s][j][h], (s + 8 * h + 128 - (EDGE - 1) * side) % 128, 1
                        )
                        total = jnp.where(low == s + 8 * h, turned, total)
                pack4[stage, where, rows + j] = total

    def first_pack(i, _):
        rows = 2 * i
        gathered = [
            [[v[s, rows + j, :, pl.ds(128 * h, 128)] for h in range(2)] for j in range(2)]
            for s in range(slots)
        ]
        pack_into(0, rows, gathered)
        return 0

    lax.fori_loop(0, EDGE, first_pack, 0)
    start_all(sub_copies(0))
    start_all(rep_copies(0))

    def local_index(s, k):
        return jnp.where(near_ref[s, k] >= 0, jnp.maximum(near_ref[s, k], 0) % slots, zero_slot)

    def local_pass(src, put):
        def by_slot(s, _):
            below_three_far, below_four_far = far_sides(s)
            two_low = local_index(s, 2)
            two_high = local_index(s, 3)
            three_low = jnp.where(below_three_far, zero_slot, local_index(s, 4))
            three_high = jnp.where(below_three_far, local_index(s, 5), zero_slot)
            four = jnp.where(below_four_far, local_index(s, 7), local_index(s, 6))
            four_turn = jnp.where(below_four_far, EDGE - 1, 128 - (EDGE - 1))

            def by_one(i, _):
                rows = 2 * i
                under = jnp.where(i == 0, zero_slot, s)
                over = jnp.where(i == EDGE - 1, zero_slot, s)
                under_rows = jnp.maximum(rows - 2, 0)
                over_rows = jnp.minimum(rows + 2, 2 * EDGE - 2)
                make_four = one_c[s, i, MAKE_FOUR]
                above_one_c = one_c[s, i, ABOVE_ONE]
                out_one = one_c[s, i, OUT_ONE]
                inner_below = jnp.where(low == 0, 0.0, make_four)
                cells = [
                    [src[s, rows + j, :, pl.ds(128 * h, 128)] for h in range(2)] for j in range(2)
                ]
                for j in range(2):
                    make_three = row_c[s, MAKE_THREE, j]
                    above_two_c = row_c[s, ABOVE_TWO, j]
                    out_row = row_c[s, OUT_ROW, j] + out_one
                    before = src[three_low, rows + j, :, pl.ds(128, 128)]
                    after = src[three_high, rows + j, :, pl.ds(0, 128)]
                    left, right = cells[j]
                    up_edge = lane >= 128 - EDGE
                    down_edge = lane < EDGE
                    below_three = (
                        pltpu.roll(jnp.where(up_edge, before, left), EDGE, 1),
                        pltpu.roll(jnp.where(up_edge, left, right), EDGE, 1),
                    )
                    above_three = (
                        pltpu.roll(jnp.where(down_edge, right, left), 128 - EDGE, 1),
                        pltpu.roll(jnp.where(down_edge, after, right), 128 - EDGE, 1),
                    )
                    for h in range(2):
                        cols = pl.ds(128 * h, 128)
                        here = cells[j][h]
                        if j == 0:
                            lower = src[two_low, rows + 1, :, cols]
                            upper = cells[1][h]
                        else:
                            lower = cells[0][h]
                            upper = src[two_high, rows, :, cols]
                        below_two = pltpu.roll(jnp.where(sublane == 7, lower, here), 1, 0)
                        above_two = pltpu.roll(jnp.where(sublane == 0, upper, here), 7, 0)
                        across = pltpu.roll(src[four, rows + j, :, cols], four_turn, 1)
                        total = make_three * below_three[h]
                        total += lane_c[s, ABOVE_THREE, :, cols] * above_three[h]
                        total += lane_c[s, BELOW_ONE, :, cols] * src[under, under_rows + j, :, cols]
                        total += above_one_c * src[over, over_rows + j, :, cols]
                        total += lane_c[s, BELOW_TWO, :, cols] * below_two
                        total += above_two_c * above_two
                        total += inner_below * pltpu.roll(here, 1, 1)
                        total += lane_c[s, ABOVE_FOUR, :, cols] * pltpu.roll(here, 127, 1)
                        total += (
                            make_four * lane_c[s, LOCAL_BELOW, :, cols]
                            + lane_c[s, LOCAL_ABOVE, :, cols]
                        ) * across
                        total -= (out_row + lane_c[s, OUT_LANE, :, cols]) * here
                        put(s, rows + j, cols, here, total)
                return 0

            lax.fori_loop(0, EDGE, by_one, 0)
            return 0

        lax.fori_loop(0, slots, by_slot, 0)

    def far_turns(s):
        below_three_far, below_four_far = far_sides(s)
        three = jnp.maximum(jnp.where(below_three_far, near_ref[s, 4], near_ref[s, 5]), 0) % slots
        four = jnp.maximum(jnp.where(below_four_far, near_ref[s, 6], near_ref[s, 7]), 0) % slots
        three_turn = (jnp.where(below_three_far, 128, 128 + 128 - EDGE) - EDGE * three) % 128
        four_turn = jnp.where(below_four_far, 128, 128 + EDGE - 1) - four
        three_side = jnp.where(below_three_far, 0, 1) if sub_count > 2 else 0
        four_side = jnp.where(below_four_far, 0, 1) if rep_count > 2 else 0
        return three_side, three_turn, four_side, four_turn % 128, (four_turn - 8) % 128

    def far_terms(stage, s, i, turns):
        three_side, three_turn, four_side, turn_left, turn_right = turns
        rows = 2 * i
        make_four = one_c[s, i, MAKE_FOUR]
        terms = []
        for j in range(2):
            third = pltpu.roll(far3[stage][three_side, rows + j], three_turn, 1)
            fourth = far4[stage][four_side, rows + j]
            halves = []
            for h, turn in ((0, turn_left), (1, turn_right)):
                cols = pl.ds(128 * h, 128)
                weight = (
                    make_four * lane_c[s, FAR_BELOW_FOUR, :, cols]
                    + lane_c[s, FAR_ABOVE_FOUR, :, cols]
                )
                edge = (
                    row_c[s, MAKE_THREE, j] * lane_c[s, FAR_BELOW_THREE, :, cols]
                    if h == 0
                    else lane_c[s, FAR_ABOVE_THREE, :, cols]
                )
                term = jnp.where(edge != 0.0, edge * third, 0.0)
                term += jnp.where(weight != 0.0, weight * pltpu.roll(fourth, turn, 1), 0.0)
                halves.append(term)
            terms.append(halves)
        return terms

    def first_terms(stage, s, cols, j):
        under = jnp.maximum(near_ref[s, 0], 0) % slots
        over = jnp.maximum(near_ref[s, 1], 0) % slots
        below = lane_c[s, BELOW_ONE, :, cols] * far1[stage][0, under, j, :, cols]
        above = one_c[s, EDGE - 1, ABOVE_ONE] * far1[stage][1, over, j, :, cols]
        return (
            jnp.where(near_ref[s, 0] >= 0, below, 0.0),
            jnp.where(near_ref[s, 1] >= 0, above, 0.0),
        )

    def add_first(stage, target, scale):
        def by_slot(s, _):
            for j in range(2):
                for h in range(2):
                    cols = pl.ds(128 * h, 128)
                    below, above = first_terms(stage, s, cols, j)
                    target[s, j, :, cols] += scale * below
                    target[s, 2 * EDGE - 2 + j, :, cols] += scale * above
            return 0

        lax.fori_loop(0, slots, by_slot, 0)

    def put_middle(s, row, cols, here, total):
        m[s, row, :, cols] = here + total

    local_pass(v, put_middle)

    arrivals(own_copies(0, x_ref), True)
    add_first(0, m, 1.0)
    arrivals(sub_copies(0), True)
    arrivals(rep_copies(0), True)

    def second_pack(i, _):
        rows = 2 * i
        gathered = []
        for s in range(slots):
            terms = far_terms(0, s, i, far_turns(s))
            tile = []
            for j in range(2):
                halves = []
                for h in range(2):
                    cols = pl.ds(128 * h, 128)
                    cells = m[s, rows + j, :, cols] + terms[j][h]
                    m[s, rows + j, :, cols] = cells
                    halves.append(cells)
                tile.append(halves)
            gathered.append(tile)
        pack_into(1, rows, gathered)
        return 0

    lax.fori_loop(0, EDGE, second_pack, 0)
    start_all(own_copies(1, m))
    start_all(sub_copies(1))
    start_all(rep_copies(1))

    def put_next(s, row, cols, here, total):
        y[s, row, :, cols] = 0.5 * (v[s, row, :, cols] + here + total)

    local_pass(m, put_next)

    arrivals(own_copies(1, m), True)
    add_first(1, y, 0.5)
    arrivals(sub_copies(1), True)
    arrivals(rep_copies(1), True)

    stores = [
        pltpu.make_async_copy(y.at[s], out_ref.at[s], store_sem.at[s]) for s in range(slots)
    ]
    for s in range(slots):
        turns = far_turns(s)
        active = coord_ref[s, 0] >= 0

        def by_one(i, _):
            rows = 2 * i
            terms = far_terms(1, s, i, turns)
            for j in range(2):
                for h in range(2):
                    cols = pl.ds(128 * h, 128)
                    cells = y[s, rows + j, :, cols] + 0.5 * terms[j][h]
                    y[s, rows + j, :, cols] = jnp.where(active, cells, 0.0)
            return 0

        lax.fori_loop(0, EDGE, by_one, 0)
        stores[s].start()
    for stage, source in ((0, x_ref), (1, m)):
        finish(own_copies(stage, source))
        finish(sub_copies(stage))
        finish(rep_copies(stage))
    for copy in stores:
        copy.wait()


def solution(mesh):
    counts = tuple(mesh.shape[axis] for axis in ("own", "sub", "rep"))

    def on_device(density, tile_coords, neighbours, rate_constants):
        slots, area, _ = density.shape
        cells = density.reshape(slots, area // 8, 8, area)
        tile = (slots + 1, area // 8, 8, area)
        face = (2, 2, area // 8, 8, 128)
        smem = pl.BlockSpec(memory_space=pltpu.SMEM)
        dma = pltpu.SemaphoreType.DMA
        out = pl.pallas_call(
            functools.partial(kernel, counts),
            out_shape=jax.ShapeDtypeStruct(cells.shape, F32),
            in_specs=[pl.BlockSpec(memory_space=pl.ANY), smem, smem, smem],
            out_specs=pl.BlockSpec(memory_space=pl.ANY),
            scratch_shapes=[
                pltpu.VMEM(tile, F32),
                pltpu.VMEM(tile, F32),
                pltpu.VMEM(cells.shape, F32),
                pltpu.VMEM((slots, LANE_ROWS, 8, area), F32),
                pltpu.VMEM((slots, 3, 2, 8, 128), F32),
                pltpu.VMEM((slots, EDGE, 3, 8, 128), F32),
                pltpu.VMEM(face, F32),
                pltpu.VMEM(face, F32),
                *[pltpu.VMEM((2, slots, 2, 8, area), F32)] * 2,
                *[pltpu.VMEM(face[1:], F32)] * 4,
                dma((slots,)),
                dma((slots,)),
                dma((2, 2)),
                dma((2, 2)),
                dma((2, 2)),
                dma((2, 2)),
                dma((2, 2)),
                dma((2, 2)),
            ],
            compiler_params=pltpu.CompilerParams(
                collective_id=0, has_side_effects=True, vmem_limit_bytes=40 << 20
            ),
        )(cells, tile_coords, neighbours, rate_constants)
        return out.reshape(density.shape)

    spec = P(("parts", "own", "sub", "rep"), None)
    cube = P(("parts", "own", "sub", "rep"), None, None)
    return jax.shard_map(
        on_device, mesh=mesh, in_specs=(cube, spec, spec, P("parts")), out_specs=cube, check_vma=False
    )
```

```python
import functools

import jax
import jax.numpy as jnp
from jax import lax
from jax.experimental import pallas as pl
from jax.experimental.pallas import tpu as pltpu
from jax.sharding import PartitionSpec as P

C_DEV = 2
D_DEV = 2
N1 = 512
N2 = 512
N3 = 256
N4 = 256
EDGE = 16
F32 = jnp.float32
MESH = pl.DeviceIdType.MESH

BELOW_ONE, ABOVE_THREE, BELOW_TWO, ABOVE_FOUR, OUT_LANE, LOCAL_ABOVE, LOCAL_BELOW = range(7)
FAR_ABOVE_FOUR, FAR_BELOW_FOUR, FAR_ABOVE_THREE, FAR_BELOW_THREE = range(7, 11)
LANE_ROWS = 11
MAKE_THREE, ABOVE_TWO, OUT_ROW = range(3)
MAKE_FOUR, ABOVE_ONE, OUT_ONE = range(3)


def kernel(counts, x_ref, coord_hbm, near_hbm, rate_hbm, out_ref,
           coord_ref, near_ref, rate_ref, small_sem, v, m, y, lane_c, row_c, one_c, pack3, pack4, far1_a, far1_b, far3_a, far3_b, far4_a, far4_b,
           load_sem, store_sem, send1, recv1, send3, recv3, send4, recv4):
    slots = x_ref.shape[0]
    zero_slot = slots
    far1, far3, far4 = (far1_a, far1_b), (far3_a, far3_b), (far4_a, far4_b)
    own_count, sub_count, rep_count = counts
    own = lax.axis_index("own")
    sub = lax.axis_index("sub")
    rep = lax.axis_index("rep")

    loads = [
        pltpu.make_async_copy(x_ref.at[s], v.at[s], load_sem.at[s]) for s in range(slots)
    ]
    for copy in loads:
        copy.start()

    small = [
        pltpu.make_async_copy(source, held, small_sem.at[k])
        for k, (source, held) in enumerate(
            ((coord_hbm, coord_ref), (near_hbm, near_ref), (rate_hbm, rate_ref))
        )
    ]
    for copy in small:
        copy.start()

    barrier = pltpu.get_barrier_semaphore()
    expected = jnp.int32(0)
    for axis, index, count in (("own", own, own_count), ("sub", sub, sub_count), ("rep", rep, rep_count)):
        for step, there in ((-1, index > 0), (1, index < count - 1)):
            expected = expected + there.astype(jnp.int32)

            @pl.when(there)
            def _():
                pl.semaphore_signal(
                    barrier, inc=1, device_id={axis: index + step}, device_id_type=MESH
                )

    def own_copies(stage, source):
        down = pltpu.make_async_remote_copy(
            src_ref=source.at[pl.ds(0, slots), pl.ds(0, 2)],
            dst_ref=far1[stage].at[1],
            send_sem=send1.at[stage, 0],
            recv_sem=recv1.at[stage, 1],
            device_id={"own": own - 1},
            device_id_type=MESH,
        )
        up = pltpu.make_async_remote_copy(
            src_ref=source.at[pl.ds(0, slots), pl.ds(2 * EDGE - 2, 2)],
            dst_ref=far1[stage].at[0],
            send_sem=send1.at[stage, 1],
            recv_sem=recv1.at[stage, 0],
            device_id={"own": own + 1},
            device_id_type=MESH,
        )
        return (down, own > 0), (up, own < own_count - 1)

    def face_copies(stage, axis, index, count, pack, far, send, recv):
        if count == 2:
            return (
                (
                    pltpu.make_async_remote_copy(
                        src_ref=pack.at[stage, 0],
                        dst_ref=far[stage].at[0],
                        send_sem=send.at[stage, 0],
                        recv_sem=recv.at[stage, 0],
                        device_id={axis: 1 - index},
                        device_id_type=MESH,
                    ),
                    index >= 0,
                ),
            )
        return tuple(
            (
                pltpu.make_async_remote_copy(
                    src_ref=pack.at[stage, side],
                    dst_ref=far[stage].at[1 - side],
                    send_sem=send.at[stage, side],
                    recv_sem=recv.at[stage, 1 - side],
                    device_id={axis: index + 2 * side - 1},
                    device_id_type=MESH,
                ),
                index > 0 if side == 0 else index < count - 1,
            )
            for side in (0, 1)
        )

    def start_all(copies):
        for copy, there in copies:

            @pl.when(there)
            def _():
                copy.start()

    def sub_copies(stage):
        return face_copies(stage, "sub", sub, sub_count, pack3, far3, send3, recv3)

    def rep_copies(stage):
        return face_copies(stage, "rep", rep, rep_count, pack4, far4, send4, recv4)

    def finish(copies):
        for copy, there in copies:

            @pl.when(there)
            def _():
                copy.wait_send()

    def arrivals(copies, flip):
        order = copies[::-1] if flip and len(copies) == 2 else copies
        for (copy, _), (_, there) in zip(order, copies):

            @pl.when(there)
            def _():
                copy.wait_recv()

    lane = lax.broadcasted_iota(jnp.int32, (8, 128), 1)
    sublane = lax.broadcasted_iota(jnp.int32, (8, 128), 0)
    low = lane % EDGE
    for copy in small:
        copy.wait()
    rate = [rate_ref[k] for k in range(10)]

    v[zero_slot] = jnp.zeros(v.shape[1:], F32)
    m[zero_slot] = jnp.zeros(m.shape[1:], F32)

    def far_sides(s):
        below_three_far = coord_ref[s, 2] % C_DEV == 0
        below_four_far = coord_ref[s, 3] % D_DEV == 0
        return below_three_far, below_four_far

    def flag(value):
        return jnp.where(value, 1.0, 0.0)

    def coefficients(s, _):
        base = [(coord_ref[s, k] * EDGE).astype(F32) for k in range(4)]
        below_three_far, below_four_far = far_sides(s)
        there = [near_ref[s, k] >= 0 for k in range(8)]
        far_below_three = flag(below_three_far & there[4])
        far_above_three = flag(jnp.logical_not(below_three_far) & there[5])
        far_below_four = flag(below_four_far & there[6])
        far_above_four = flag(jnp.logical_not(below_four_far) & there[7])
        local_below = flag(jnp.logical_not(below_four_far) & there[6])
        local_above = flag(below_four_far & there[7])
        level_four = base[3] + low.astype(F32)
        above_four = rate[6] * ((level_four + 1.0) * (1.0 / N4))
        for h in range(2):
            level_three = base[2] + (lane // EDGE + 8 * h).astype(F32)
            share_three = level_three * (1.0 / N3)
            share_four = level_four * (1.0 / N4)
            above_three = rate[1] * ((level_three + 1.0) * (1.0 / N3))
            cols = pl.ds(128 * h, 128)
            lane_c[s, BELOW_ONE, :, cols] = rate[2] * share_three
            lane_c[s, ABOVE_THREE, :, cols] = above_three
            lane_c[s, BELOW_TWO, :, cols] = rate[7] * share_four
            lane_c[s, ABOVE_FOUR, :, cols] = jnp.where(low == EDGE - 1, 0.0, above_four)
            lane_c[s, OUT_LANE, :, cols] = (
                rate[1] * share_three + rate[2] * share_three
                + rate[6] * share_four + rate[7] * share_four
            )
            lane_c[s, LOCAL_ABOVE, :, cols] = jnp.where(low == EDGE - 1, above_four, 0.0) * local_above
            lane_c[s, LOCAL_BELOW, :, cols] = jnp.where(low == 0, local_below, 0.0)
            lane_c[s, FAR_ABOVE_FOUR, :, cols] = (
                jnp.where(low == EDGE - 1, above_four, 0.0) * far_above_four
            )
            lane_c[s, FAR_BELOW_FOUR, :, cols] = jnp.where(low == 0, far_below_four, 0.0)
            lane_c[s, FAR_ABOVE_THREE, :, cols] = (
                jnp.where(lane >= 128 - EDGE, above_three, 0.0) * far_above_three
            )
            lane_c[s, FAR_BELOW_THREE, :, cols] = jnp.where(lane < EDGE, far_below_three, 0.0)
        for j in range(2):
            level_two = base[1] + (sublane + 8 * j).astype(F32)
            share_two = level_two * (1.0 / N2)
            ratio_two = share_two / rate[4]
            make_three = rate[0] / (1.0 + ratio_two * ratio_two)
            row_c[s, MAKE_THREE, j] = make_three
            row_c[s, ABOVE_TWO, j] = rate[8] * ((level_two + 1.0) * (1.0 / N2))
            row_c[s, OUT_ROW, j] = make_three + rate[8] * share_two

        def by_one(i, _):
            level_one = jnp.full((8, 128), base[0] + i.astype(F32), F32)
            share_one = level_one * (1.0 / N1)
            ratio_one = share_one / rate[9]
            make_four = rate[5] / (1.0 + ratio_one * ratio_one)
            one_c[s, i, MAKE_FOUR] = make_four
            one_c[s, i, ABOVE_ONE] = rate[3] * ((level_one + 1.0) * (1.0 / N1))
            one_c[s, i, OUT_ONE] = make_four + rate[3] * share_one
            return 0

        lax.fori_loop(0, EDGE, by_one, 0)
        return 0

    lax.fori_loop(0, slots, coefficients, 0)

    pl.semaphore_wait(barrier, expected)
    start_all(own_copies(0, x_ref))
    for copy in loads:
        copy.wait()

    def sides_of(index, count):
        return ((0, (index == 0).astype(jnp.int32)),) if count == 2 else ((0, 0), (1, 1))

    def pack_into(stage, rows, gathered):
        for where, side in sides_of(sub, sub_count):
            for j in range(2):
                total = jnp.zeros((8, 128), F32)
                for s in range(slots):
                    cells = jnp.where(side == 1, gathered[s][j][1], gathered[s][j][0])
                    turned = pltpu.roll(cells, (EDGE * s + EDGE * side) % 128, 1)
                    total = jnp.where(lane // EDGE == s, turned, total)
                pack3[stage, where, rows + j] = total
        for where, side in sides_of(rep, rep_count):
            for j in range(2):
                total = jnp.zeros((8, 128), F32)
                for s in range(slots):
                    for h in range(2):
                        turned = pltpu.roll(
                            gathered[s][j][h], (s + 8 * h + 128 - (EDGE - 1) * side) % 128, 1
                        )
                        total = jnp.where(low == s + 8 * h, turned, total)
                pack4[stage, where, rows + j] = total

    def first_pack(i, _):
        rows = 2 * i
        gathered = [
            [[v[s, rows + j, :, pl.ds(128 * h, 128)] for h in range(2)] for j in range(2)]
            for s in range(slots)
        ]
        pack_into(0, rows, gathered)
        return 0

    lax.fori_loop(0, EDGE, first_pack, 0)
    start_all(sub_copies(0))
    start_all(rep_copies(0))

    def local_index(s, k):
        return jnp.where(near_ref[s, k] >= 0, jnp.maximum(near_ref[s, k], 0) % slots, zero_slot)

    def local_pass(src, put):
        def by_slot(s, _):
            below_three_far, below_four_far = far_sides(s)
            two_low = local_index(s, 2)
            two_high = local_index(s, 3)
            three_low = jnp.where(below_three_far, zero_slot, local_index(s, 4))
            three_high = jnp.where(below_three_far, local_index(s, 5), zero_slot)
            four = jnp.where(below_four_far, local_index(s, 7), local_index(s, 6))
            four_turn = jnp.where(below_four_far, EDGE - 1, 128 - (EDGE - 1))

            def by_one(i, _):
                rows = 2 * i
                under = jnp.where(i == 0, zero_slot, s)
                over = jnp.where(i == EDGE - 1, zero_slot, s)
                under_rows = jnp.maximum(rows - 2, 0)
                over_rows = jnp.minimum(rows + 2, 2 * EDGE - 2)
                make_four = one_c[s, i, MAKE_FOUR]
                above_one_c = one_c[s, i, ABOVE_ONE]
                out_one = one_c[s, i, OUT_ONE]
                inner_below = jnp.where(low == 0, 0.0, make_four)
                cells = [
                    [src[s, rows + j, :, pl.ds(128 * h, 128)] for h in range(2)] for j in range(2)
                ]
                for j in range(2):
                    make_three = row_c[s, MAKE_THREE, j]
                    above_two_c = row_c[s, ABOVE_TWO, j]
                    out_row = row_c[s, OUT_ROW, j] + out_one
                    before = src[three_low, rows + j, :, pl.ds(128, 128)]
                    after = src[three_high, rows + j, :, pl.ds(0, 128)]
                    left, right = cells[j]
                    up_edge = lane >= 128 - EDGE
                    down_edge = lane < EDGE
                    below_three = (
                        pltpu.roll(jnp.where(up_edge, before, left), EDGE, 1),
                        pltpu.roll(jnp.where(up_edge, left, right), EDGE, 1),
                    )
                    above_three = (
                        pltpu.roll(jnp.where(down_edge, right, left), 128 - EDGE, 1),
                        pltpu.roll(jnp.where(down_edge, after, right), 128 - EDGE, 1),
                    )
                    for h in range(2):
                        cols = pl.ds(128 * h, 128)
                        here = cells[j][h]
                        if j == 0:
                            lower = src[two_low, rows + 1, :, cols]
                            upper = cells[1][h]
                        else:
                            lower = cells[0][h]
                            upper = src[two_high, rows, :, cols]
                        below_two = pltpu.roll(jnp.where(sublane == 7, lower, here), 1, 0)
                        above_two = pltpu.roll(jnp.where(sublane == 0, upper, here), 7, 0)
                        across = pltpu.roll(src[four, rows + j, :, cols], four_turn, 1)
                        total = make_three * below_three[h]
                        total += lane_c[s, ABOVE_THREE, :, cols] * above_three[h]
                        total += lane_c[s, BELOW_ONE, :, cols] * src[under, under_rows + j, :, cols]
                        total += above_one_c * src[over, over_rows + j, :, cols]
                        total += lane_c[s, BELOW_TWO, :, cols] * below_two
                        total += above_two_c * above_two
                        total += inner_below * pltpu.roll(here, 1, 1)
                        total += lane_c[s, ABOVE_FOUR, :, cols] * pltpu.roll(here, 127, 1)
                        total += (
                            make_four * lane_c[s, LOCAL_BELOW, :, cols]
                            + lane_c[s, LOCAL_ABOVE, :, cols]
                        ) * across
                        total -= (out_row + lane_c[s, OUT_LANE, :, cols]) * here
                        put(s, rows + j, cols, here, total)
                return 0

            lax.fori_loop(0, EDGE, by_one, 0, unroll=4)
            return 0

        lax.fori_loop(0, slots, by_slot, 0)

    def far_turns(s):
        below_three_far, below_four_far = far_sides(s)
        three = jnp.maximum(jnp.where(below_three_far, near_ref[s, 4], near_ref[s, 5]), 0) % slots
        four = jnp.maximum(jnp.where(below_four_far, near_ref[s, 6], near_ref[s, 7]), 0) % slots
        three_turn = (jnp.where(below_three_far, 128, 128 + 128 - EDGE) - EDGE * three) % 128
        four_turn = jnp.where(below_four_far, 128, 128 + EDGE - 1) - four
        three_side = jnp.where(below_three_far, 0, 1) if sub_count > 2 else 0
        four_side = jnp.where(below_four_far, 0, 1) if rep_count > 2 else 0
        return three_side, three_turn, four_side, four_turn % 128, (four_turn - 8) % 128

    def far_terms(stage, s, i, turns):
        three_side, three_turn, four_side, turn_left, turn_right = turns
        rows = 2 * i
        make_four = one_c[s, i, MAKE_FOUR]
        terms = []
        for j in range(2):
            third = pltpu.roll(far3[stage][three_side, rows + j], three_turn, 1)
            fourth = far4[stage][four_side, rows + j]
            halves = []
            for h, turn in ((0, turn_left), (1, turn_right)):
                cols = pl.ds(128 * h, 128)
                weight = (
                    make_four * lane_c[s, FAR_BELOW_FOUR, :, cols]
                    + lane_c[s, FAR_ABOVE_FOUR, :, cols]
                )
                edge = (
                    row_c[s, MAKE_THREE, j] * lane_c[s, FAR_BELOW_THREE, :, cols]
                    if h == 0
                    else lane_c[s, FAR_ABOVE_THREE, :, cols]
                )
                term = jnp.where(edge != 0.0, edge * third, 0.0)
                term += jnp.where(weight != 0.0, weight * pltpu.roll(fourth, turn, 1), 0.0)
                halves.append(term)
            terms.append(halves)
        return terms

    def first_terms(stage, s, cols, j):
        under = jnp.maximum(near_ref[s, 0], 0) % slots
        over = jnp.maximum(near_ref[s, 1], 0) % slots
        below = lane_c[s, BELOW_ONE, :, cols] * far1[stage][0, under, j, :, cols]
        above = one_c[s, EDGE - 1, ABOVE_ONE] * far1[stage][1, over, j, :, cols]
        return (
            jnp.where(near_ref[s, 0] >= 0, below, 0.0),
            jnp.where(near_ref[s, 1] >= 0, above, 0.0),
        )

    def add_first(stage, target, scale):
        def by_slot(s, _):
            for j in range(2):
                for h in range(2):
                    cols = pl.ds(128 * h, 128)
                    below, above = first_terms(stage, s, cols, j)
                    target[s, j, :, cols] += scale * below
                    target[s, 2 * EDGE - 2 + j, :, cols] += scale * above
            return 0

        lax.fori_loop(0, slots, by_slot, 0)

    def put_middle(s, row, cols, here, total):
        m[s, row, :, cols] = here + total

    local_pass(v, put_middle)

    arrivals(own_copies(0, x_ref), True)
    add_first(0, m, 1.0)
    arrivals(sub_copies(0), True)
    arrivals(rep_copies(0), True)

    def second_pack(i, _):
        rows = 2 * i
        gathered = []
        for s in range(slots):
            terms = far_terms(0, s, i, far_turns(s))
            tile = []
            for j in range(2):
                halves = []
                for h in range(2):
                    cols = pl.ds(128 * h, 128)
                    cells = m[s, rows + j, :, cols] + terms[j][h]
                    m[s, rows + j, :, cols] = cells
                    halves.append(cells)
                tile.append(halves)
            gathered.append(tile)
        pack_into(1, rows, gathered)
        return 0

    lax.fori_loop(0, EDGE, second_pack, 0)
    start_all(own_copies(1, m))
    start_all(sub_copies(1))
    start_all(rep_copies(1))

    def put_next(s, row, cols, here, total):
        y[s, row, :, cols] = 0.5 * (v[s, row, :, cols] + here + total)

    local_pass(m, put_next)

    arrivals(own_copies(1, m), True)
    add_first(1, y, 0.5)
    arrivals(sub_copies(1), True)
    arrivals(rep_copies(1), True)

    stores = [
        pltpu.make_async_copy(y.at[s], out_ref.at[s], store_sem.at[s]) for s in range(slots)
    ]
    for s in range(slots):
        turns = far_turns(s)
        active = coord_ref[s, 0] >= 0

        def by_one(i, _):
            rows = 2 * i
            terms = far_terms(1, s, i, turns)
            for j in range(2):
                for h in range(2):
                    cols = pl.ds(128 * h, 128)
                    cells = y[s, rows + j, :, cols] + 0.5 * terms[j][h]
                    y[s, rows + j, :, cols] = jnp.where(active, cells, 0.0)
            return 0

        lax.fori_loop(0, EDGE, by_one, 0, unroll=8)
        stores[s].start()
    for stage, source in ((0, x_ref), (1, m)):
        finish(own_copies(stage, source))
        finish(sub_copies(stage))
        finish(rep_copies(stage))
    for copy in stores:
        copy.wait()


def solution(mesh):
    counts = tuple(mesh.shape[axis] for axis in ("own", "sub", "rep"))

    def on_device(density, tile_coords, neighbours, rate_constants):
        slots, area, _ = density.shape
        cells = density.reshape(slots, area // 8, 8, area)
        tile = (slots + 1, area // 8, 8, area)
        face = (2, 2, area // 8, 8, 128)
        dma = pltpu.SemaphoreType.DMA
        out = pl.pallas_call(
            functools.partial(kernel, counts),
            out_shape=jax.ShapeDtypeStruct(cells.shape, F32),
            in_specs=[pl.BlockSpec(memory_space=pl.ANY)] * 4,
            out_specs=pl.BlockSpec(memory_space=pl.ANY),
            scratch_shapes=[
                pltpu.SMEM(tile_coords.shape, jnp.int32),
                pltpu.SMEM(neighbours.shape, jnp.int32),
                pltpu.SMEM(rate_constants.shape, F32),
                dma((3,)),
                pltpu.VMEM(tile, F32),
                pltpu.VMEM(tile, F32),
                pltpu.VMEM(cells.shape, F32),
                pltpu.VMEM((slots, LANE_ROWS, 8, area), F32),
                pltpu.VMEM((slots, 3, 2, 8, 128), F32),
                pltpu.VMEM((slots, EDGE, 3, 8, 128), F32),
                pltpu.VMEM(face, F32),
                pltpu.VMEM(face, F32),
                *[pltpu.VMEM((2, slots, 2, 8, area), F32)] * 2,
                *[pltpu.VMEM(face[1:], F32)] * 4,
                dma((slots,)),
                dma((slots,)),
                dma((2, 2)),
                dma((2, 2)),
                dma((2, 2)),
                dma((2, 2)),
                dma((2, 2)),
                dma((2, 2)),
            ],
            compiler_params=pltpu.CompilerParams(
                collective_id=0, has_side_effects=True, vmem_limit_bytes=62 << 20
            ),
        )(cells, tile_coords, neighbours, rate_constants)
        return out.reshape(density.shape)

    spec = P(("parts", "own", "sub", "rep"), None)
    cube = P(("parts", "own", "sub", "rep"), None, None)
    return jax.shard_map(
        on_device, mesh=mesh, in_specs=(cube, spec, spec, P("parts")), out_specs=cube, check_vma=False
    )
```

```python
import functools

import jax
import jax.numpy as jnp
from jax import lax
from jax.experimental import pallas as pl
from jax.experimental.pallas import tpu as pltpu
from jax.sharding import PartitionSpec as P

C_DEV = 2
D_DEV = 2
N1 = 512
N2 = 512
N3 = 256
N4 = 256
EDGE = 16
F32 = jnp.float32
MESH = pl.DeviceIdType.MESH
PIECES = 4
PIECE = EDGE // PIECES

BELOW_ONE, ABOVE_THREE, BELOW_TWO, ABOVE_FOUR, OUT_LANE, LOCAL_ABOVE, LOCAL_BELOW = range(7)
FAR_ABOVE_FOUR, FAR_BELOW_FOUR, FAR_ABOVE_THREE, FAR_BELOW_THREE = range(7, 11)
LANE_ROWS = 11
MAKE_THREE, ABOVE_TWO, OUT_ROW = range(3)
MAKE_FOUR, ABOVE_ONE, OUT_ONE = range(3)


def kernel(counts, x_ref, coord_hbm, near_hbm, rate_hbm, y,
           coord_ref, near_ref, rate_ref, turn_ref, small_sem, v, m, lane_c, row_c, one_c, pack3, pack4, far1_a, far1_b, far3_a, far3_b, far4_a, far4_b,
           load_sem, send1, recv1, send3, recv3, send4, recv4):
    slots = x_ref.shape[0]
    zero_slot = slots
    far1, far3, far4 = (far1_a, far1_b), (far3_a, far3_b), (far4_a, far4_b)
    own_count, sub_count, rep_count = counts
    own = lax.axis_index("own")
    sub = lax.axis_index("sub")
    rep = lax.axis_index("rep")

    loads = [
        pltpu.make_async_copy(x_ref.at[s], v.at[s], load_sem.at[s]) for s in range(slots)
    ]
    for copy in loads:
        copy.start()

    small = [
        pltpu.make_async_copy(source, held, small_sem.at[k])
        for k, (source, held) in enumerate(
            ((coord_hbm, coord_ref), (near_hbm, near_ref), (rate_hbm, rate_ref))
        )
    ]
    for copy in small:
        copy.start()

    for count, far in ((sub_count, far3), (rep_count, far4)):
        if count > 2:
            for held in far:
                held[...] = jnp.zeros_like(held)

    barrier = pltpu.get_barrier_semaphore()
    expected = jnp.int32(0)
    for axis, index, count in (("own", own, own_count), ("sub", sub, sub_count), ("rep", rep, rep_count)):
        for step, there in ((-1, index > 0), (1, index < count - 1)):
            expected = expected + there.astype(jnp.int32)

            @pl.when(there)
            def _():
                pl.semaphore_signal(
                    barrier, inc=1, device_id={axis: index + step}, device_id_type=MESH
                )

    def own_copies(stage, source):
        down = pltpu.make_async_remote_copy(
            src_ref=source.at[pl.ds(0, slots), pl.ds(0, 2)],
            dst_ref=far1[stage].at[1],
            send_sem=send1.at[stage, 0],
            recv_sem=recv1.at[stage, 1],
            device_id={"own": own - 1},
            device_id_type=MESH,
        )
        up = pltpu.make_async_remote_copy(
            src_ref=source.at[pl.ds(0, slots), pl.ds(2 * EDGE - 2, 2)],
            dst_ref=far1[stage].at[0],
            send_sem=send1.at[stage, 1],
            recv_sem=recv1.at[stage, 0],
            device_id={"own": own + 1},
            device_id_type=MESH,
        )
        return (down, own > 0), (up, own < own_count - 1)

    def face_copies(stage, axis, index, count, pack, far, send, recv, piece):
        rows = pl.ds(2 * PIECE * piece, 2 * PIECE)
        copies = []
        for side in (0,) if count == 2 else (0, 1):
            land = 0 if count == 2 else 1 - side
            copies.append(
                (
                    pltpu.make_async_remote_copy(
                        src_ref=pack.at[stage, side, rows],
                        dst_ref=far[stage].at[land, rows],
                        send_sem=send.at[stage, side, piece],
                        recv_sem=recv.at[stage, land, piece],
                        device_id={axis: 1 - index if count == 2 else index + 2 * side - 1},
                        device_id_type=MESH,
                    ),
                    index >= 0 if count == 2 else index > 0 if side == 0 else index < count - 1,
                )
            )
        return tuple(copies)

    def start_all(copies):
        for copy, there in copies:

            @pl.when(there)
            def _():
                copy.start()

    def sub_copies(stage, piece):
        return face_copies(stage, "sub", sub, sub_count, pack3, far3, send3, recv3, piece)

    def rep_copies(stage, piece):
        return face_copies(stage, "rep", rep, rep_count, pack4, far4, send4, recv4, piece)

    def tile_rows(p):
        return jnp.where(p == 0, 0, jnp.where(p == 1, EDGE - 1, p - 1))

    def finish(copies):
        for copy, there in copies:

            @pl.when(there)
            def _():
                copy.wait_send()

    def arrivals(copies, flip):
        order = copies[::-1] if flip and len(copies) == 2 else copies
        for (copy, _), (_, there) in zip(order, copies):

            @pl.when(there)
            def _():
                copy.wait_recv()

    lane = lax.broadcasted_iota(jnp.int32, (8, 128), 1)
    sublane = lax.broadcasted_iota(jnp.int32, (8, 128), 0)
    low = lane % EDGE
    for copy in small:
        copy.wait()
    rate = [rate_ref[k] for k in range(10)]

    v[zero_slot] = jnp.zeros(v.shape[1:], F32)
    m[zero_slot] = jnp.zeros(m.shape[1:], F32)

    def far_sides(s):
        below_three_far = coord_ref[2, s] % C_DEV == 0
        below_four_far = coord_ref[3, s] % D_DEV == 0
        return below_three_far, below_four_far

    def flag(value):
        return jnp.where(value, 1.0, 0.0)

    def far_turns(s):
        below_three_far, below_four_far = far_sides(s)
        three = jnp.maximum(jnp.where(below_three_far, near_ref[s, 4], near_ref[s, 5]), 0) % slots
        four = jnp.maximum(jnp.where(below_four_far, near_ref[s, 6], near_ref[s, 7]), 0) % slots
        three_turn = (jnp.where(below_three_far, 128, 128 + 128 - EDGE) - EDGE * three) % 128
        four_turn = jnp.where(below_four_far, 128, 128 + EDGE - 1) - four
        three_side = jnp.where(below_three_far, 0, 1) if sub_count > 2 else 0
        four_side = jnp.where(below_four_far, 0, 1) if rep_count > 2 else 0
        return three_side, three_turn, four_side, four_turn % 128, (four_turn - 8) % 128

    def coefficients(s, _):
        base = [(coord_ref[k, s] * EDGE).astype(F32) for k in range(4)]
        below_three_far, below_four_far = far_sides(s)
        there = [near_ref[s, k] >= 0 for k in range(8)]
        far_below_three = flag(below_three_far & there[4])
        far_above_three = flag(jnp.logical_not(below_three_far) & there[5])
        far_below_four = flag(below_four_far & there[6])
        far_above_four = flag(jnp.logical_not(below_four_far) & there[7])
        local_below = flag(jnp.logical_not(below_four_far) & there[6])
        local_above = flag(below_four_far & there[7])
        level_four = base[3] + low.astype(F32)
        above_four = rate[6] * ((level_four + 1.0) * (1.0 / N4))
        for h in range(2):
            level_three = base[2] + (lane // EDGE + 8 * h).astype(F32)
            share_three = level_three * (1.0 / N3)
            share_four = level_four * (1.0 / N4)
            above_three = rate[1] * ((level_three + 1.0) * (1.0 / N3))
            cols = pl.ds(128 * h, 128)
            lane_c[s, BELOW_ONE, :, cols] = rate[2] * share_three
            lane_c[s, ABOVE_THREE, :, cols] = above_three
            lane_c[s, BELOW_TWO, :, cols] = rate[7] * share_four
            lane_c[s, ABOVE_FOUR, :, cols] = jnp.where(low == EDGE - 1, 0.0, above_four)
            lane_c[s, OUT_LANE, :, cols] = (
                rate[1] * share_three + rate[2] * share_three
                + rate[6] * share_four + rate[7] * share_four
            )
            lane_c[s, LOCAL_ABOVE, :, cols] = jnp.where(low == EDGE - 1, above_four, 0.0) * local_above
            lane_c[s, LOCAL_BELOW, :, cols] = jnp.where(low == 0, local_below, 0.0)
            lane_c[s, FAR_ABOVE_FOUR, :, cols] = (
                jnp.where(low == EDGE - 1, above_four, 0.0) * far_above_four
            )
            lane_c[s, FAR_BELOW_FOUR, :, cols] = jnp.where(low == 0, far_below_four, 0.0)
            lane_c[s, FAR_ABOVE_THREE, :, cols] = (
                jnp.where(lane >= 128 - EDGE, above_three, 0.0) * far_above_three
            )
            lane_c[s, FAR_BELOW_THREE, :, cols] = jnp.where(lane < EDGE, far_below_three, 0.0)
        for j in range(2):
            level_two = base[1] + (sublane + 8 * j).astype(F32)
            share_two = level_two * (1.0 / N2)
            ratio_two = share_two / rate[4]
            make_three = rate[0] / (1.0 + ratio_two * ratio_two)
            row_c[s, MAKE_THREE, j] = make_three
            row_c[s, ABOVE_TWO, j] = rate[8] * ((level_two + 1.0) * (1.0 / N2))
            row_c[s, OUT_ROW, j] = make_three + rate[8] * share_two

        def by_one(i, _):
            level_one = jnp.full((8, 128), base[0] + i.astype(F32), F32)
            share_one = level_one * (1.0 / N1)
            ratio_one = share_one / rate[9]
            make_four = rate[5] / (1.0 + ratio_one * ratio_one)
            one_c[s, i, MAKE_FOUR] = make_four
            one_c[s, i, ABOVE_ONE] = rate[3] * ((level_one + 1.0) * (1.0 / N1))
            one_c[s, i, OUT_ONE] = make_four + rate[3] * share_one
            return 0

        lax.fori_loop(0, EDGE, by_one, 0)
        for k, turn in enumerate(far_turns(s)):
            turn_ref[s, k] = jnp.int32(turn)
        return 0

    lax.fori_loop(0, slots, coefficients, 0)

    pl.semaphore_wait(barrier, expected)
    start_all(own_copies(0, x_ref))
    for copy in loads:
        copy.wait()

    def sides_of(index, count):
        return ((0, (index == 0).astype(jnp.int32)),) if count == 2 else ((0, 0), (1, 1))

    def pack_into(stage, rows, gathered):
        for where, side in sides_of(sub, sub_count):
            for j in range(2):
                total = jnp.zeros((8, 128), F32)
                for s in range(slots):
                    cells = jnp.where(side == 1, gathered[s][j][1], gathered[s][j][0])
                    turned = pltpu.roll(cells, (EDGE * s + EDGE * side) % 128, 1)
                    total = jnp.where(lane // EDGE == s, turned, total)
                pack3[stage, where, rows + j] = total
        for where, side in sides_of(rep, rep_count):
            for j in range(2):
                total = jnp.zeros((8, 128), F32)
                for s in range(slots):
                    for h in range(2):
                        turned = pltpu.roll(
                            gathered[s][j][h], (s + 8 * h + 128 - (EDGE - 1) * side) % 128, 1
                        )
                        total = jnp.where(low == s + 8 * h, turned, total)
                pack4[stage, where, rows + j] = total

    def first_pack(p, _):
        rows = 2 * tile_rows(p)
        gathered = [
            [[v[s, rows + j, :, pl.ds(128 * h, 128)] for h in range(2)] for j in range(2)]
            for s in range(slots)
        ]
        pack_into(0, 2 * p, gathered)
        return 0

    for piece in range(PIECES):
        lax.fori_loop(PIECE * piece, PIECE * (piece + 1), first_pack, 0, unroll=2)
        start_all(sub_copies(0, piece))
        start_all(rep_copies(0, piece))

    def local_index(s, k):
        return jnp.where(near_ref[s, k] >= 0, jnp.maximum(near_ref[s, k], 0) % slots, zero_slot)

    def local_pass(src, put):
        def by_slot(s, _):
            below_three_far, below_four_far = far_sides(s)
            two_low = local_index(s, 2)
            two_high = local_index(s, 3)
            three_low = jnp.where(below_three_far, zero_slot, local_index(s, 4))
            three_high = jnp.where(below_three_far, local_index(s, 5), zero_slot)
            four = jnp.where(below_four_far, local_index(s, 7), local_index(s, 6))
            four_turn = jnp.where(below_four_far, EDGE - 1, 128 - (EDGE - 1))

            def by_one(i, _):
                rows = 2 * i
                under = jnp.where(i == 0, zero_slot, s)
                over = jnp.where(i == EDGE - 1, zero_slot, s)
                under_rows = jnp.maximum(rows - 2, 0)
                over_rows = jnp.minimum(rows + 2, 2 * EDGE - 2)
                make_four = one_c[s, i, MAKE_FOUR]
                above_one_c = one_c[s, i, ABOVE_ONE]
                out_one = one_c[s, i, OUT_ONE]
                inner_below = jnp.where(low == 0, 0.0, make_four)
                cells = [
                    [src[s, rows + j, :, pl.ds(128 * h, 128)] for h in range(2)] for j in range(2)
                ]
                for j in range(2):
                    make_three = row_c[s, MAKE_THREE, j]
                    above_two_c = row_c[s, ABOVE_TWO, j]
                    out_row = row_c[s, OUT_ROW, j] + out_one
                    before = src[three_low, rows + j, :, pl.ds(128, 128)]
                    after = src[three_high, rows + j, :, pl.ds(0, 128)]
                    left, right = cells[j]
                    up_edge = lane >= 128 - EDGE
                    down_edge = lane < EDGE
                    below_three = (
                        pltpu.roll(jnp.where(up_edge, before, left), EDGE, 1),
                        pltpu.roll(jnp.where(up_edge, left, right), EDGE, 1),
                    )
                    above_three = (
                        pltpu.roll(jnp.where(down_edge, right, left), 128 - EDGE, 1),
                        pltpu.roll(jnp.where(down_edge, after, right), 128 - EDGE, 1),
                    )
                    for h in range(2):
                        cols = pl.ds(128 * h, 128)
                        here = cells[j][h]
                        if j == 0:
                            lower = src[two_low, rows + 1, :, cols]
                            upper = cells[1][h]
                        else:
                            lower = cells[0][h]
                            upper = src[two_high, rows, :, cols]
                        below_two = pltpu.roll(jnp.where(sublane == 7, lower, here), 1, 0)
                        above_two = pltpu.roll(jnp.where(sublane == 0, upper, here), 7, 0)
                        across = pltpu.roll(src[four, rows + j, :, cols], four_turn, 1)
                        total = make_three * below_three[h]
                        total += lane_c[s, ABOVE_THREE, :, cols] * above_three[h]
                        total += lane_c[s, BELOW_ONE, :, cols] * src[under, under_rows + j, :, cols]
                        total += above_one_c * src[over, over_rows + j, :, cols]
                        total += lane_c[s, BELOW_TWO, :, cols] * below_two
                        total += above_two_c * above_two
                        total += inner_below * pltpu.roll(here, 1, 1)
                        total += lane_c[s, ABOVE_FOUR, :, cols] * pltpu.roll(here, 127, 1)
                        total += (
                            make_four * lane_c[s, LOCAL_BELOW, :, cols]
                            + lane_c[s, LOCAL_ABOVE, :, cols]
                        ) * across
                        total -= (out_row + lane_c[s, OUT_LANE, :, cols]) * here
                        put(s, rows + j, cols, here, total)
                return 0

            lax.fori_loop(0, EDGE, by_one, 0, unroll=16)
            return 0

        lax.fori_loop(0, slots, by_slot, 0)

    def far_terms(stage, s, p, i):
        three_side = turn_ref[s, 0] if sub_count > 2 else 0
        four_side = turn_ref[s, 2] if rep_count > 2 else 0
        three_turn = turn_ref[s, 1]
        rows = 2 * p
        make_four = one_c[s, i, MAKE_FOUR]
        terms = []
        for j in range(2):
            third = pltpu.roll(far3[stage][three_side, rows + j], three_turn, 1)
            fourth = far4[stage][four_side, rows + j]
            halves = []
            for h in range(2):
                cols = pl.ds(128 * h, 128)
                weight = (
                    make_four * lane_c[s, FAR_BELOW_FOUR, :, cols]
                    + lane_c[s, FAR_ABOVE_FOUR, :, cols]
                )
                edge = (
                    row_c[s, MAKE_THREE, j] * lane_c[s, FAR_BELOW_THREE, :, cols]
                    if h == 0
                    else lane_c[s, FAR_ABOVE_THREE, :, cols]
                )
                halves.append(edge * third + weight * pltpu.roll(fourth, turn_ref[s, 3 + h], 1))
            terms.append(halves)
        return terms

    def first_terms(stage, s, cols, j):
        under = jnp.maximum(near_ref[s, 0], 0) % slots
        over = jnp.maximum(near_ref[s, 1], 0) % slots
        below = lane_c[s, BELOW_ONE, :, cols] * far1[stage][0, under, j, :, cols]
        above = one_c[s, EDGE - 1, ABOVE_ONE] * far1[stage][1, over, j, :, cols]
        return (
            jnp.where(near_ref[s, 0] >= 0, below, 0.0),
            jnp.where(near_ref[s, 1] >= 0, above, 0.0),
        )

    def add_first(stage, target, scale):
        def by_slot(s, _):
            for j in range(2):
                for h in range(2):
                    cols = pl.ds(128 * h, 128)
                    below, above = first_terms(stage, s, cols, j)
                    target[s, j, :, cols] += scale * below
                    target[s, 2 * EDGE - 2 + j, :, cols] += scale * above
            return 0

        lax.fori_loop(0, slots, by_slot, 0)

    def put_middle(s, row, cols, here, total):
        m[s, row, :, cols] = here + total

    local_pass(v, put_middle)

    arrivals(own_copies(0, x_ref), True)
    add_first(0, m, 1.0)

    def second_pack(p, _):
        i = tile_rows(p)
        rows = 2 * i
        gathered = []
        for s in range(slots):
            terms = far_terms(0, s, p, i)
            tile = []
            for j in range(2):
                halves = []
                for h in range(2):
                    cols = pl.ds(128 * h, 128)
                    cells = m[s, rows + j, :, cols] + terms[j][h]
                    m[s, rows + j, :, cols] = cells
                    halves.append(cells)
                tile.append(halves)
            gathered.append(tile)
        pack_into(1, 2 * p, gathered)
        return 0

    for piece in range(PIECES):
        arrivals(sub_copies(0, piece), True)
        arrivals(rep_copies(0, piece), True)
        lax.fori_loop(PIECE * piece, PIECE * (piece + 1), second_pack, 0, unroll=2)
        if piece == 0:
            start_all(own_copies(1, m))
        start_all(sub_copies(1, piece))
        start_all(rep_copies(1, piece))

    def put_next(s, row, cols, here, total):
        y[s, row, :, cols] = 0.5 * (v[s, row, :, cols] + here + total)

    local_pass(m, put_next)

    arrivals(own_copies(1, m), True)
    add_first(1, y, 0.5)

    def last_terms(p, _):
        i = tile_rows(p)
        rows = 2 * i
        for s in range(slots):
            active = coord_ref[0, s] >= 0
            terms = far_terms(1, s, p, i)
            for j in range(2):
                for h in range(2):
                    cols = pl.ds(128 * h, 128)
                    cells = y[s, rows + j, :, cols] + 0.5 * terms[j][h]
                    y[s, rows + j, :, cols] = jnp.where(active, cells, 0.0)
        return 0

    for piece in range(PIECES):
        arrivals(sub_copies(1, piece), True)
        arrivals(rep_copies(1, piece), True)
        lax.fori_loop(PIECE * piece, PIECE * (piece + 1), last_terms, 0, unroll=2)
    for stage, source in ((0, x_ref), (1, m)):
        finish(own_copies(stage, source))
        for piece in range(PIECES):
            finish(sub_copies(stage, piece))
            finish(rep_copies(stage, piece))


def solution(mesh):
    counts = tuple(mesh.shape[axis] for axis in ("own", "sub", "rep"))

    def on_device(density, tile_coords, neighbours, rate_constants):
        slots, area, _ = density.shape
        cells = density.reshape(slots, area // 8, 8, area)
        tile = (slots + 1, area // 8, 8, area)
        face = (2, 2, area // 8, 8, 128)
        dma = pltpu.SemaphoreType.DMA
        out = pl.pallas_call(
            functools.partial(kernel, counts),
            out_shape=jax.ShapeDtypeStruct(cells.shape, F32),
            in_specs=[pl.BlockSpec(memory_space=pl.ANY)] * 4,
            out_specs=pl.BlockSpec(memory_space=pltpu.VMEM),
            scratch_shapes=[
                pltpu.SMEM(tile_coords.shape[::-1], jnp.int32),
                pltpu.SMEM(neighbours.shape, jnp.int32),
                pltpu.SMEM(rate_constants.shape, F32),
                pltpu.SMEM((slots, 5), jnp.int32),
                dma((3,)),
                pltpu.VMEM(tile, F32),
                pltpu.VMEM(tile, F32),
                pltpu.VMEM((slots, LANE_ROWS, 8, area), F32),
                pltpu.VMEM((slots, 3, 2, 8, 128), F32),
                pltpu.VMEM((slots, EDGE, 3, 8, 128), F32),
                pltpu.VMEM(face, F32),
                pltpu.VMEM(face, F32),
                *[pltpu.VMEM((2, slots, 2, 8, area), F32)] * 2,
                *[pltpu.VMEM(face[1:], F32)] * 4,
                dma((slots,)),
                dma((2, 2)),
                dma((2, 2)),
                dma((2, 2, PIECES)),
                dma((2, 2, PIECES)),
                dma((2, 2, PIECES)),
                dma((2, 2, PIECES)),
            ],
            compiler_params=pltpu.CompilerParams(
                collective_id=0, has_side_effects=True, vmem_limit_bytes=62 << 20
            ),
        )(cells, tile_coords.T, neighbours, rate_constants)
        return out.reshape(density.shape)

    spec = P(("parts", "own", "sub", "rep"), None)
    cube = P(("parts", "own", "sub", "rep"), None, None)
    return jax.shard_map(
        on_device, mesh=mesh, in_specs=(cube, spec, spec, P("parts")), out_specs=cube, check_vma=False
    )
```
